32 devices in a mesh: tensor: 8 (over y, x, core), seq: 4 (over z).
Axes of the slice: x: 2, y: 2, z: 4, core: 2. Of those that a mesh axis runs over, the one named last changes fastest.
Arguments:
- resid: bfloat16 [4, 128, 2048], P('seq', 'tensor'), may hold values from -6 to 6
- norm_gain: bfloat16 [2048], replicated, may hold values from 0.099609375 to 1.8984375
- gate_weight_matrix: bfloat16 [2048, 10944], P(None, 'tensor'), may hold values from -0.125 to 0.125
- up_weight: bfloat16 [2048, 10944], P(None, 'tensor'), may hold values from -0.125 to 0.125
- w_down: bfloat16 [10944, 2048], P('tensor'), may hold values from -0.0546875 to 0.0546875
- gate_a: bfloat16 [16, 2048, 16], P('seq', 'tensor'), may hold values from -0.125 to 0.125
- gate_b: bfloat16 [16, 16, 10944], P('seq', None, 'tensor'), may hold values from -1.5 to 1.5
- up_a: bfloat16 [16, 2048, 16], P('seq', 'tensor'), may hold values from -0.125 to 0.125
- up_b: bfloat16 [16, 16, 10944], P('seq', None, 'tensor'), may hold values from -1.5 to 1.5
- down_a: bfloat16 [16, 10944, 16], P('seq', 'tensor'), may hold values from -0.0546875 to 0.0546875
- down_b: bfloat16 [16, 16, 2048], P('seq'), may hold values from -1.5 to 1.5
- prompt_lengths: int32 [4, 8], P('seq'), may hold values from 1 to 64, 128 in all within a row
- prompt_choice: int32 [4, 8], P('seq'), may hold values from 0 to 15
- used_adapters: int32 [16], replicated, may hold values from 0 to 15, as said below
- adapter_holder: int32 [16], replicated, may hold values from 0 to 15, each once
Outputs:
- output: bfloat16 [4, 128, 2048], P('seq', 'tensor')
The draws below stay inside these ranges and needn't reach their ends.
Inputs may be any that keep to these rules, and one draw needn't show every extreme that they name: `used_adapters`: 16 distinct adapter ids.
All inputs are finite; a program needn't handle non-finite values.
Results may differ from the reference program's by a relative error of at most 0.017.
Values may be sent and summed in bfloat16 or wider, within the bound.
A program may use at most 128 MiB of HBM per device.

```python
import math
import jax
import jax.numpy as jnp
import numpy as np
from jax import lax

D = 2048
FF = 10944
RANK = 16
USED = 16
PROMPTS = 8
GROUP_TOK = 128
LONGEST = 64
GROUPS = 4
ADAPTERS = 16
N_TENSOR = 8


def draw_used_adapters(key, part):
    first_key = jax.random.fold_in(key, 11)
    second_key = jax.random.fold_in(key, 12)
    middle = 1 + jax.random.permutation(first_key, ADAPTERS - 2)[:USED - 2]
    corners = jnp.array([0, ADAPTERS - 1], jnp.int32)
    whole = jnp.concatenate([corners, middle.astype(jnp.int32)])
    order = jax.random.permutation(second_key, USED)
    return whole[order]


def touch_ends(values, stream_key, least, largest):
    longest = values.shape.index(max(values.shape))
    spots = []
    for shift in (0, 1):
        where = [jax.random.randint(jax.random.fold_in(stream_key, axis), (), 0, length) for axis, length in enumerate(values.shape)]
        where[longest] = (where[longest] + shift) % values.shape[longest]
        spots.append(tuple(where))
    return values.at[spots[0]].set(least).at[spots[1]].set(largest)


def block_levels(stream_key, shape, shards, low, top_value):
    def one(position, parts):
        steps = jax.random.uniform(jax.random.fold_in(jax.random.fold_in(stream_key, 6), position), (parts,), jnp.float32, low / len(shards), top_value / len(shards))
        return jnp.repeat(jnp.exp(steps), shape[position] // parts).reshape((-1,) + (1,) * (len(shape) - position - 1))

    gain = one(*shards[0])
    for cut in shards[1:]:
        gain = gain * one(*cut)
    return gain


def length_profile(number_of, total, reach, skew):
    loads = [(1 << 20) // math.isqrt(grade ** skew) + 1 for grade in range(2, number_of + 1)]
    surplus, given = total - reach - (number_of - 1), [1] * (number_of - 1)
    while surplus > 0:
        candidates = [i for i in range(number_of - 1) if given[i] < reach]
        pool, left = sum([loads[i] for i in candidates]), surplus
        for i in candidates:
            more = min(reach - given[i], max(1, left * loads[i] // pool), surplus)
            given[i] = given[i] + more
            surplus = surplus - more
    return np.array([reach] + given)


def ragged_sizes(own_key, amount, total, bound, lean):
    if amount == 2:
        one = jax.random.randint(own_key, (), max(1, total - bound), min(bound, total - 1) + 1)
        return jnp.stack([one, total - one])
    sizes = jnp.asarray(length_profile(amount, total, bound, lean), jnp.int32)
    pairs = (amount - 1) // 2
    giver, receiver = sizes[1:1 + 2 * pairs:2], sizes[2:2 + 2 * pairs:2]
    room = jnp.minimum(giver - 1, bound - receiver)
    passed = jax.random.randint(jax.random.fold_in(own_key, 1), (pairs,), 0, 1 << 20) % (room + 1)
    sizes = sizes.at[1:1 + 2 * pairs:2].set(giver - passed).at[2:2 + 2 * pairs:2].set(receiver + passed)
    return sizes[jax.random.permutation(jax.random.fold_in(own_key, 2), amount)]


def normal_values(rng, extent, width, bound, pieces=(), kind=jnp.bfloat16):
    factor_of = block_levels(rng, extent, pieces, -0.22, 0.18) if pieces else 1.0
    values = jax.random.normal(rng, extent, jnp.float32) * width * factor_of
    return jnp.minimum(jnp.maximum(values, -bound), bound).astype(kind)


def setup_inputs(seed: int = 0) -> dict:
    arg_keys = jax.random.split(jax.random.key(seed), 16)
    return {
        "resid": normal_values(arg_keys[0], (GROUPS, GROUP_TOK, D), 1.0, 6.0, ((0, 4), (1, 8))),
        "norm_gain": jnp.clip(1.0 + 0.18 * jax.random.normal(arg_keys[1], (D,), jnp.float32), 0.099609375, 1.8984375).astype(jnp.bfloat16),
        "gate_weight_matrix": normal_values(arg_keys[2], (D, FF), D ** -0.5, 0.125, ((1, 8),)),
        "up_weight": normal_values(arg_keys[3], (D, FF), D ** -0.5, 0.125, ((1, 8),)),
        "w_down": normal_values(arg_keys[4], (FF, D), FF ** -0.5, 0.0546875, ((0, 8),)),
        "gate_a": normal_values(arg_keys[5], (ADAPTERS, D, RANK), D ** -0.5, 0.125, ((0, 4), (1, 8))),
        "gate_b": normal_values(arg_keys[6], (ADAPTERS, RANK, FF), RANK ** -0.5, 1.5, ((0, 4), (2, 8))),
        "up_a": normal_values(arg_keys[7], (ADAPTERS, D, RANK), D ** -0.5, 0.125, ((0, 4), (1, 8))),
        "up_b": normal_values(arg_keys[8], (ADAPTERS, RANK, FF), RANK ** -0.5, 1.5, ((0, 4), (2, 8))),
        "down_a": normal_values(arg_keys[9], (ADAPTERS, FF, RANK), FF ** -0.5, 0.0546875, ((0, 4), (1, 8))),
        "down_b": normal_values(arg_keys[10], (ADAPTERS, RANK, D), RANK ** -0.5, 1.5, ((0, 4),)),
        "prompt_lengths": jax.vmap(lambda own: ragged_sizes(own, PROMPTS, GROUP_TOK, LONGEST, 2))(jax.random.split(arg_keys[11], GROUPS)).reshape((GROUPS, PROMPTS)).astype(jnp.int32),
        "prompt_choice": touch_ends(jax.random.randint(arg_keys[12], (GROUPS, PROMPTS), 0, USED), jax.random.fold_in(arg_keys[12], 1), 0, USED - 1).astype(jnp.int32),
        "used_adapters": draw_used_adapters(jax.random.fold_in(arg_keys[15], 71), 0),
        "adapter_holder": jax.random.permutation(arg_keys[14], ADAPTERS).astype(jnp.int32),
    }


adapter_scale = 0.5

def token_choice(lengths, choices):
    prompt_ends = jnp.cumsum(lengths)
    positions = jnp.arange(GROUP_TOK, dtype=jnp.int32)
    prompt_index = lax.optimization_barrier(jnp.sum((positions[:, None] >= prompt_ends[None, :]).astype(jnp.int32), axis=1))
    hits = prompt_index[:, None] == jnp.arange(PROMPTS, dtype=jnp.int32)[None, :]
    return lax.optimization_barrier(jnp.sum(jnp.where(hits, choices[None, :], 0), axis=1)).astype(jnp.int32)

def reference(resid, norm_gain, gate_weight_matrix, up_weight, w_down, gate_a, gate_b, up_a, up_b, down_a, down_b, prompt_lengths, prompt_choice, used_adapters, adapter_holder):
    slot_used = adapter_holder[used_adapters]
    gate_in = jnp.transpose(gate_a[slot_used], (1, 0, 2)).reshape(D, USED * RANK)
    up_in = jnp.transpose(up_a[slot_used], (1, 0, 2)).reshape(D, USED * RANK)
    down_in = jnp.transpose(down_a[slot_used], (1, 0, 2)).reshape(FF, USED * RANK)
    gate_output = gate_b[slot_used].reshape(USED * RANK, FF)
    up_output = up_b[slot_used].reshape(USED * RANK, FF)
    down_output = down_b[slot_used].reshape(USED * RANK, D)
    block_width = FF // N_TENSOR
    down_blocks = w_down.astype(jnp.float32).reshape(N_TENSOR, block_width, D)
    gain_f = norm_gain.astype(jnp.float32)

    def select(low_rank, weights):
        picked = lax.optimization_barrier(jnp.sum(low_rank.reshape(GROUP_TOK, USED, RANK) * weights[:, :, None], axis=1)).astype(jnp.bfloat16)
        spread = (picked[:, None, :].astype(jnp.float32) * weights[:, :, None]).astype(jnp.bfloat16)
        return spread.reshape(GROUP_TOK, USED * RANK)

    def one_group(inputs):
        resid_g, lengths, choices = inputs
        weights = (token_choice(lengths, choices)[:, None] == jnp.arange(USED, dtype=jnp.int32)[None, :]).astype(jnp.float32)
        residual_float = resid_g.astype(jnp.float32)
        scale = lax.rsqrt(lax.optimization_barrier(jnp.mean(residual_float * residual_float, axis=-1, keepdims=True)) + 1e-06)
        normalized_input = (residual_float * scale * gain_f).astype(jnp.bfloat16)
        gate_adapter_rows = select(jnp.dot(normalized_input, gate_in, preferred_element_type=jnp.float32), weights)
        up_adapter_rows = select(jnp.dot(normalized_input, up_in, preferred_element_type=jnp.float32), weights)
        gate_preactivation = jnp.dot(normalized_input, gate_weight_matrix, preferred_element_type=jnp.float32) + adapter_scale * jnp.dot(gate_adapter_rows, gate_output, preferred_element_type=jnp.float32)
        up_preactivation = jnp.dot(normalized_input, up_weight, preferred_element_type=jnp.float32) + adapter_scale * jnp.dot(up_adapter_rows, up_output, preferred_element_type=jnp.float32)
        hidden = (jax.nn.silu(gate_preactivation) * up_preactivation).astype(jnp.bfloat16)
        hidden_blocks = hidden.astype(jnp.float32).reshape(GROUP_TOK, N_TENSOR, block_width)
        partials = jnp.einsum('tkf,kfd->ktd', hidden_blocks, down_blocks, precision=lax.Precision.HIGHEST)
        partials = lax.optimization_barrier(partials.astype(jnp.bfloat16))
        down_total_sum = lax.optimization_barrier(jnp.sum(partials.astype(jnp.float32), axis=0))
        down_adapter_rows = select(jnp.dot(hidden, down_in, preferred_element_type=jnp.float32), weights)
        adapter_down_term = jnp.dot(down_adapter_rows, down_output, preferred_element_type=jnp.float32)
        return (residual_float + down_total_sum + adapter_scale * adapter_down_term).astype(jnp.bfloat16)
    return lax.map(one_group, (resid, prompt_lengths, prompt_choice))
```

```python
import functools

import jax
import jax.numpy as jnp
from jax import lax
from jax.experimental import pallas as pl
from jax.experimental.pallas import tpu as pltpu
from jax.sharding import PartitionSpec as P

adapter_scale = 0.5
MESH = pl.DeviceIdType.MESH
COL_TILE = 256
SUM_CHUNKS = 4
NT = (((1,), (1,)), ((), ()))
NN = (((1,), (0,)), ((), ()))


def mm(a, b, dims):
    return lax.dot_general(a, b, dims, preferred_element_type=jnp.float32)


def tiles(width, body):
    full = width // COL_TILE

    def step(i, carry):
        body(pl.ds(pl.multiple_of(i * COL_TILE, COL_TILE), COL_TILE))
        return carry

    if full:
        lax.fori_loop(0, full, step, 0)
    if width % COL_TILE:
        body(pl.ds(full * COL_TILE, width % COL_TILE))


def kernel(
    tensor_n,
    pair_n,
    resid_ref,
    gain_ref,
    wg_hbm,
    wu_hbm,
    wd_hbm,
    ga_ref,
    gb_ref,
    ua_ref,
    ub_ref,
    da_ref,
    db_ref,
    lengths_ref,
    choice_ref,
    used_ref,
    holder_ref,
    out_ref,
    wg,
    wu,
    wd,
    x,
    ga,
    gb,
    ua,
    ub,
    da,
    db,
    slots_own,
    slots_far,
    mid_own,
    mid_in,
    pre_g,
    pre_u,
    hidden,
    y,
    y_in,
    z_out,
    z_in,
    kept,
    w_sem,
    own_sem,
    x_send,
    x_recv,
    far_send,
    far_recv,
    ad_send,
    ad_recv,
    mid_send,
    mid_recv,
    y_send,
    y_recv,
):
    k = lax.axis_index("tensor")
    s = lax.axis_index("seq")
    half = s // pair_n
    place = lax.rem(s, pair_n)
    far = {"seq": (1 - half) * pair_n + place}
    tok_dev, width = resid_ref.shape
    group_tok = tok_dev * tensor_n
    toks = 2 * group_tok
    stored_rows, hidden_local = gb_ref.shape
    rank_n = mid_own.shape[0] // 2
    rows = pair_n * stored_rows
    slots_n = rows // rank_n
    feat_loc = ga_ref.shape[1]
    chunk = width // SUM_CHUNKS

    def peer(d):
        return {"tensor": lax.rem(k + d, tensor_n)}

    def mate(d):
        return {"seq": half * pair_n + lax.rem(place + d, pair_n)}

    weights = [
        pltpu.make_async_copy(wg_hbm, wg, w_sem.at[0]),
        pltpu.make_async_copy(wu_hbm, wu, w_sem.at[1]),
        pltpu.make_async_copy(wd_hbm, wd, w_sem.at[2]),
    ]
    for copy in weights:
        copy.start()
    pairs = [(ga_ref, ga), (ua_ref, ua), (gb_ref, gb), (ub_ref, ub), (da_ref, da), (db_ref, db)]
    own_copies = [
        pltpu.make_async_copy(src, dst.at[place], own_sem.at[i])
        for i, (src, dst) in enumerate(pairs)
    ]
    for copy in own_copies:
        copy.start()

    barrier = pltpu.get_barrier_semaphore()
    for d in range(1, tensor_n):
        pl.semaphore_signal(barrier, inc=1, device_id=peer(d), device_id_type=MESH)
    for d in range(1, pair_n):
        pl.semaphore_signal(barrier, inc=1, device_id=mate(d), device_id_type=MESH)
    pl.semaphore_signal(barrier, inc=1, device_id=far, device_id_type=MESH)

    res = resid_ref[...].astype(jnp.float32)
    scale = lax.rsqrt(jnp.mean(res * res, axis=-1, keepdims=True) + 1e-06)
    x[0, k] = (res * scale * gain_ref[...].astype(jnp.float32)).astype(jnp.bfloat16)

    position = lax.broadcasted_iota(jnp.int32, (8, group_tok), 1)
    slot_line = jnp.zeros((8, group_tok), jnp.float32)
    end = jnp.int32(0)
    for p in range(lengths_ref.shape[1]):
        slot = holder_ref[used_ref[choice_ref[0, p]]]
        first, end = end, end + lengths_ref[0, p]
        inside = jnp.logical_and(position >= first, position < end)
        slot_line = jnp.where(inside, slot.astype(jnp.float32), slot_line)
    slots_own[...] = slot_line

    pl.semaphore_wait(barrier, tensor_n - 1 + pair_n - 1 + 1)

    sends = []

    def remote(src, dst, send_sem, recv_sem, device):
        copy = pltpu.make_async_remote_copy(
            src_ref=src,
            dst_ref=dst,
            send_sem=send_sem,
            recv_sem=recv_sem,
            device_id=device,
            device_id_type=MESH,
        )
        return copy

    def send(*args):
        copy = remote(*args)
        copy.start()
        sends.append(copy)

    send(x.at[0, k], x.at[1, k], far_send.at[0], far_recv.at[0], far)
    for d in range(1, tensor_n):
        send(x.at[0, k], x.at[0, k], x_send.at[0, d - 1], x_recv.at[0, d - 1], peer(d))
    send(slots_own, slots_far, far_send.at[1], far_recv.at[1], far)
    for i, (src, dst) in enumerate(pairs):
        for d in range(1, pair_n):
            send(src, dst.at[place], ad_send.at[i, d - 1], ad_recv.at[i, d - 1], mate(d))

    def wait_pair(i):
        own_copies[i].wait()
        src, dst = pairs[i]
        for d in range(1, pair_n):
            origin = lax.rem(place - d + pair_n, pair_n)
            remote(
                src, dst.at[origin], ad_send.at[i, d - 1], ad_recv.at[i, d - 1], mate(d)
            ).wait_recv()

    remote(x.at[0, k], x.at[1, k], far_send.at[0], far_recv.at[0], far).wait_recv()
    for d in range(1, tensor_n):
        send(x.at[1, k], x.at[1, k], x_send.at[1, d - 1], x_recv.at[1, d - 1], peer(d))
    for h in range(2):
        for d in range(1, tensor_n):
            origin = lax.rem(k - d + tensor_n, tensor_n)
            remote(
                x.at[h, k], x.at[h, origin], x_send.at[h, d - 1], x_recv.at[h, d - 1], peer(d)
            ).wait_recv()
    remote(slots_own, slots_far, far_send.at[1], far_recv.at[1], far).wait_recv()

    base = (half * (pair_n * (stored_rows // rank_n))).astype(jnp.float32)
    line = jnp.concatenate([slots_own[...], slots_far[...]], axis=1) - base
    line_rows = jnp.broadcast_to(line[0:1, :], (rows, toks))
    row_slot = (lax.broadcasted_iota(jnp.int32, (rows, toks), 0) // rank_n).astype(jnp.float32)
    mask_t = line_rows == row_slot

    wait_pair(0)
    wait_pair(1)
    copies = max(1, 128 // feat_loc)
    span = copies * feat_loc
    mine = x[:, :, :, pl.ds(pl.multiple_of(k // copies * span, span), span)].reshape(toks, span)
    for i, a_ref in enumerate((ga, ua)):
        a = a_ref[...].reshape(rows, feat_loc)
        if copies > 1:
            a = jnp.concatenate([a] * copies, axis=1)
            part = lax.broadcasted_iota(jnp.int32, (rows, span), 1) // feat_loc
            a = jnp.where(part == lax.rem(k, copies), a, jnp.zeros_like(a))
        low = mm(a, mine, NT)
        low = jnp.where(mask_t, low, 0.0).reshape(slots_n, rank_n, toks)
        mid_own[pl.ds(i * rank_n, rank_n), :] = jnp.sum(low, axis=0).astype(jnp.bfloat16)
    for d in range(1, tensor_n):
        send(mid_own, mid_in.at[d - 1], mid_send.at[d - 1], mid_recv.at[d - 1], peer(d))

    weights[0].wait()
    weights[1].wait()

    def project(cols):
        block = x[...].reshape(toks, width)
        pre_g[:, cols] = mm(block, wg[cols, :], NT)
        pre_u[:, cols] = mm(block, wu[cols, :], NT)

    tiles(hidden_local, project)

    mid = mid_own[...].astype(jnp.float32)
    for d in range(1, tensor_n):
        remote(
            mid_own, mid_in.at[d - 1], mid_send.at[d - 1], mid_recv.at[d - 1], peer(d)
        ).wait_recv()
        mid = mid + mid_in[d - 1].astype(jnp.float32)
    mid = mid.astype(jnp.bfloat16).astype(jnp.float32)
    spreads = []
    for i in range(2):
        part = mid[i * rank_n : (i + 1) * rank_n][None]
        part = jnp.broadcast_to(part, (slots_n, rank_n, toks)).reshape(rows, toks)
        part = jnp.where(mask_t, adapter_scale * part, 0.0)
        spreads.append(part.T.astype(jnp.bfloat16))
    slot_cols = line_rows[: min(rows, 128)].T[:, 0:1]
    held = jnp.logical_and(slot_cols >= 0.0, slot_cols < float(slots_n))
    wait_pair(2)
    wait_pair(3)

    def activate(cols):
        wide = cols.size
        g = pre_g[:, cols] + mm(spreads[0], gb[:, :, cols].reshape(rows, wide), NN)
        u = pre_u[:, cols] + mm(spreads[1], ub[:, :, cols].reshape(rows, wide), NN)
        h = g / (1.0 + jnp.exp(-g)) * u
        hidden[:, cols] = jnp.where(held, h, 0.0).astype(jnp.bfloat16)

    tiles(hidden_local, activate)

    wait_pair(4)
    low = mm(hidden[...], da[...].reshape(rows, hidden_local), NT)
    col_slot = (lax.broadcasted_iota(jnp.int32, (toks, rows), 1) // rank_n).astype(jnp.float32)
    low = jnp.where(slot_cols == col_slot, adapter_scale * low, 0.0).astype(jnp.bfloat16)
    wait_pair(5)
    weights[2].wait()
    for c in range(SUM_CHUNKS):
        cols = pl.ds(c * chunk, chunk)
        part = mm(hidden[...], wd[:, cols], NN) + mm(low, db[:, :, cols].reshape(rows, chunk), NN)
        y[:, :, :, cols] = part.astype(jnp.bfloat16).reshape(2, tensor_n, tok_dev, chunk)
        for d in range(1, tensor_n):
            to = lax.rem(k + d, tensor_n)
            send(
                y.at[:, to, :, cols],
                y_in.at[d - 1, :, :, cols],
                y_send.at[c, d - 1],
                y_recv.at[c, d - 1],
                peer(d),
            )
    for c in range(SUM_CHUNKS):
        cols = pl.ds(c * chunk, chunk)
        total = y[:, k, :, cols].astype(jnp.float32)
        for d in range(1, tensor_n):
            remote(
                y.at[:, k, :, cols],
                y_in.at[d - 1, :, :, cols],
                y_send.at[c, d - 1],
                y_recv.at[c, d - 1],
                peer(d),
            ).wait_recv()
            total = total + y_in[d - 1, :, :, cols].astype(jnp.float32)
        z_out[c] = total[1].astype(jnp.bfloat16)
        send(z_out.at[c], z_in.at[c], far_send.at[2 + c], far_recv.at[2 + c], far)
        kept[:, cols] = total[0]
    for c in range(SUM_CHUNKS):
        cols = pl.ds(c * chunk, chunk)
        remote(z_out.at[c], z_in.at[c], far_send.at[2 + c], far_recv.at[2 + c], far).wait_recv()
        whole = resid_ref[:, cols].astype(jnp.float32) + kept[:, cols] + z_in[c].astype(jnp.float32)
        out_ref[:, cols] = whole.astype(jnp.bfloat16)
    for copy in sends:
        copy.wait_send()


def local(
    pair_n,
    resid,
    norm_gain,
    gate_weight_matrix,
    up_weight,
    w_down,
    gate_a,
    gate_b,
    up_a,
    up_b,
    down_a,
    down_b,
    prompt_lengths,
    prompt_choice,
    used_adapters,
    adapter_holder,
):
    tensor_n = lax.axis_size("tensor")
    _, tok_dev, width = resid.shape
    stored, feat_loc, rank_n = gate_a.shape
    hidden_local = gate_weight_matrix.shape[1]
    toks = 2 * tok_dev * tensor_n
    rows = stored * rank_n
    bf = jnp.bfloat16

    def by_row(a):
        return jnp.transpose(a, (0, 2, 1)).reshape(rows, a.shape[1])

    def flat(b):
        return b.reshape(rows, b.shape[2])

    vmem = pl.BlockSpec(memory_space=pltpu.VMEM)
    smem = pl.BlockSpec(memory_space=pltpu.SMEM)
    hbm = pl.BlockSpec(memory_space=pl.ANY)
    dma = pltpu.SemaphoreType.DMA
    chunk = width // SUM_CHUNKS
    out = pl.pallas_call(
        functools.partial(kernel, tensor_n, pair_n),
        out_shape=jax.ShapeDtypeStruct((tok_dev, width), bf),
        in_specs=[vmem, vmem, hbm, hbm, hbm] + [vmem] * 6 + [smem] * 4,
        out_specs=vmem,
        scratch_shapes=[
            pltpu.VMEM((hidden_local, width), bf),
            pltpu.VMEM((hidden_local, width), bf),
            pltpu.VMEM((hidden_local, width), bf),
            pltpu.VMEM((2, tensor_n, tok_dev, width), bf),
            pltpu.VMEM((pair_n, rows, feat_loc), bf),
            pltpu.VMEM((pair_n, rows, hidden_local), bf),
            pltpu.VMEM((pair_n, rows, feat_loc), bf),
            pltpu.VMEM((pair_n, rows, hidden_local), bf),
            pltpu.VMEM((pair_n, rows, hidden_local), bf),
            pltpu.VMEM((pair_n, rows, width), bf),
            pltpu.VMEM((8, toks // 2), jnp.float32),
            pltpu.VMEM((8, toks // 2), jnp.float32),
            pltpu.VMEM((2 * rank_n, toks), bf),
            pltpu.VMEM((tensor_n - 1, 2 * rank_n, toks), bf),
            pltpu.VMEM((toks, hidden_local), jnp.float32),
            pltpu.VMEM((toks, hidden_local), jnp.float32),
            pltpu.VMEM((toks, hidden_local), bf),
            pltpu.VMEM((2, tensor_n, tok_dev, width), bf),
            pltpu.VMEM((tensor_n - 1, 2, tok_dev, width), bf),
            pltpu.VMEM((SUM_CHUNKS, tok_dev, chunk), bf),
            pltpu.VMEM((SUM_CHUNKS, tok_dev, chunk), bf),
            pltpu.VMEM((tok_dev, width), jnp.float32),
            dma((3,)),
            dma((6,)),
            dma((2, tensor_n - 1)),
            dma((2, tensor_n - 1)),
            dma((2 + SUM_CHUNKS,)),
            dma((2 + SUM_CHUNKS,)),
            dma((6, max(1, pair_n - 1))),
            dma((6, max(1, pair_n - 1))),
            dma((tensor_n - 1,)),
            dma((tensor_n - 1,)),
            dma((SUM_CHUNKS, tensor_n - 1)),
            dma((SUM_CHUNKS, tensor_n - 1)),
        ],
        compiler_params=pltpu.CompilerParams(
            collective_id=0, has_side_effects=True, vmem_limit_bytes=60 * 2**20
        ),
        name="ffn",
    )(
        resid[0],
        norm_gain[None],
        gate_weight_matrix.T,
        up_weight.T,
        w_down,
        by_row(gate_a),
        flat(gate_b),
        by_row(up_a),
        flat(up_b),
        by_row(down_a),
        flat(down_b),
        prompt_lengths,
        prompt_choice,
        used_adapters,
        adapter_holder,
    )
    return out[None]


def solution(mesh):
    placed = (
        P("seq", "tensor", None),
        P(),
        P(None, "tensor"),
        P(None, "tensor"),
        P("tensor", None),
        P("seq", "tensor", None),
        P("seq", None, "tensor"),
        P("seq", "tensor", None),
        P("seq", None, "tensor"),
        P("seq", "tensor", None),
        P("seq", None, None),
        P("seq", None),
        P("seq", None),
        P(),
        P(),
    )
    return jax.shard_map(
        functools.partial(local, mesh.shape["seq"] // 2),
        mesh=mesh,
        in_specs=placed,
        out_specs=P("seq", "tensor", None),
        check_vma=False,
    )
```

```python
import functools

import jax
import jax.numpy as jnp
from jax import lax
from jax.experimental import pallas as pl
from jax.experimental.pallas import tpu as pltpu
from jax.sharding import PartitionSpec as P

adapter_scale = 0.5
MESH = pl.DeviceIdType.MESH
COL_TILE = 256
SUM_CHUNKS = 4
NT = (((1,), (1,)), ((), ()))
NN = (((1,), (0,)), ((), ()))


def mm(a, b, dims):
    return lax.dot_general(a, b, dims, preferred_element_type=jnp.float32)


def tiles(width, body):
    full = width // COL_TILE

    def step(i, carry):
        body(pl.ds(pl.multiple_of(i * COL_TILE, COL_TILE), COL_TILE))
        return carry

    if full:
        lax.fori_loop(0, full, step, 0)
    if width % COL_TILE:
        body(pl.ds(full * COL_TILE, width % COL_TILE))


def kernel(
    tensor_n,
    pair_n,
    resid_ref,
    gain_ref,
    wg_hbm,
    wu_hbm,
    wd_hbm,
    ga_ref,
    gb_ref,
    ua_ref,
    ub_ref,
    da_ref,
    db_ref,
    lengths_ref,
    choice_ref,
    used_ref,
    holder_ref,
    out_ref,
    wg,
    wu,
    wd,
    x,
    ga,
    gb,
    ua,
    ub,
    da,
    db,
    slots_own,
    slots_far,
    mid_own,
    mid_in,
    pre_g,
    pre_u,
    hidden,
    y,
    y_pair,
    y_sum,
    y_in,
    z_out,
    z_in,
    kept,
    w_sem,
    own_sem,
    x_send,
    x_recv,
    far_send,
    far_recv,
    ad_send,
    ad_recv,
    mid_send,
    mid_recv,
    y_send,
    y_recv,
    pair_send,
    pair_recv,
):
    k = lax.axis_index("tensor")
    s = lax.axis_index("seq")
    half = s // pair_n
    place = lax.rem(s, pair_n)
    far = {"seq": (1 - half) * pair_n + place}
    tok_dev, width = resid_ref.shape
    group_tok = tok_dev * tensor_n
    toks = 2 * group_tok
    stored_rows, hidden_local = gb_ref.shape
    rank_n = mid_own.shape[0] // 2
    rows = pair_n * stored_rows
    slots_n = rows // rank_n
    feat_loc = ga_ref.shape[1]
    chunk = width // SUM_CHUNKS

    chips = tensor_n // 2
    chip, core = k // 2, lax.rem(k, 2)
    sibling = {"tensor": chip * 2 + 1 - core}

    def peer(d):
        return {"tensor": lax.rem(k + d, tensor_n)}

    def chip_after(d):
        return lax.rem(chip + d, chips)

    def chip_before(d):
        return lax.rem(chip - d + chips, chips)

    def across(d):
        return {"tensor": chip_after(d) * 2 + core}

    def mate(d):
        return {"seq": half * pair_n + lax.rem(place + d, pair_n)}

    weights = [
        pltpu.make_async_copy(wg_hbm, wg, w_sem.at[0]),
        pltpu.make_async_copy(wu_hbm, wu, w_sem.at[1]),
        pltpu.make_async_copy(wd_hbm, wd, w_sem.at[2]),
    ]
    for copy in weights:
        copy.start()
    pairs = [(ga_ref, ga), (ua_ref, ua), (gb_ref, gb), (ub_ref, ub), (da_ref, da), (db_ref, db)]
    own_copies = [
        pltpu.make_async_copy(src, dst.at[place], own_sem.at[i])
        for i, (src, dst) in enumerate(pairs)
    ]
    for copy in own_copies:
        copy.start()

    barrier = pltpu.get_barrier_semaphore()
    for d in range(1, tensor_n):
        pl.semaphore_signal(barrier, inc=1, device_id=peer(d), device_id_type=MESH)
    for d in range(1, pair_n):
        pl.semaphore_signal(barrier, inc=1, device_id=mate(d), device_id_type=MESH)
    pl.semaphore_signal(barrier, inc=1, device_id=far, device_id_type=MESH)

    res = resid_ref[...].astype(jnp.float32)
    scale = lax.rsqrt(jnp.mean(res * res, axis=-1, keepdims=True) + 1e-06)
    x[0, k] = (res * scale * gain_ref[...].astype(jnp.float32)).astype(jnp.bfloat16)

    position = lax.broadcasted_iota(jnp.int32, (8, group_tok), 1)
    slot_line = jnp.zeros((8, group_tok), jnp.float32)
    end = jnp.int32(0)
    for p in range(lengths_ref.shape[1]):
        slot = holder_ref[used_ref[choice_ref[0, p]]]
        first, end = end, end + lengths_ref[0, p]
        inside = jnp.logical_and(position >= first, position < end)
        slot_line = jnp.where(inside, slot.astype(jnp.float32), slot_line)
    slots_own[...] = slot_line

    pl.semaphore_wait(barrier, tensor_n - 1 + pair_n - 1 + 1)

    sends = []

    def remote(src, dst, send_sem, recv_sem, device):
        copy = pltpu.make_async_remote_copy(
            src_ref=src,
            dst_ref=dst,
            send_sem=send_sem,
            recv_sem=recv_sem,
            device_id=device,
            device_id_type=MESH,
        )
        return copy

    def send(*args):
        copy = remote(*args)
        copy.start()
        sends.append(copy)

    send(x.at[0, k], x.at[1, k], far_send.at[0], far_recv.at[0], far)

    def block(h, index, j, device):
        return x.at[h, index], x.at[h, index], x_send.at[h, j], x_recv.at[h, j], device

    def spread_block(h):
        for d in range(1, chips):
            send(*block(h, k, d, across(d)))
        send(*block(h, k, 0, sibling))

    spread_block(0)
    send(slots_own, slots_far, far_send.at[1], far_recv.at[1], far)
    share = width // 2
    own_share = pl.ds(pl.multiple_of(core * share, share), share)
    other_share = pl.ds(pl.multiple_of((1 - core) * share, share), share)
    last = len(pairs) - 1
    for i, (src, dst) in enumerate(pairs[:last]):
        for d in range(1, pair_n):
            send(src, dst.at[place], ad_send.at[i, d - 1], ad_recv.at[i, d - 1], mate(d))

    def half_of(origin, d, cols):
        return (
            db_ref.at[:, cols],
            db.at[origin, :, cols],
            ad_send.at[last, d - 1],
            ad_recv.at[last, d - 1],
            mate(d),
        )

    def handed(origin, d, cols):
        return (
            db.at[origin, :, cols],
            db.at[origin, :, cols],
            ad_send.at[last + 1, d - 1],
            ad_recv.at[last + 1, d - 1],
            sibling,
        )

    for d in range(1, pair_n):
        send(*half_of(place, d, own_share))

    def wait_pair(i):
        own_copies[i].wait()
        src, dst = pairs[i]
        for d in range(1, pair_n):
            origin = lax.rem(place - d + pair_n, pair_n)
            remote(
                src, dst.at[origin], ad_send.at[i, d - 1], ad_recv.at[i, d - 1], mate(d)
            ).wait_recv()

    remote(x.at[0, k], x.at[1, k], far_send.at[0], far_recv.at[0], far).wait_recv()
    spread_block(1)
    for h in range(2):
        for d in range(1, chips):
            origin = chip_before(d) * 2 + core
            remote(*block(h, origin, d, across(d))).wait_recv()
            send(*block(h, origin, chips - 1 + d, sibling))
    for h in range(2):
        remote(*block(h, chip * 2 + 1 - core, 0, sibling)).wait_recv()
        for d in range(1, chips):
            origin = chip_before(d) * 2 + 1 - core
            remote(*block(h, origin, chips - 1 + d, sibling)).wait_recv()
    remote(slots_own, slots_far, far_send.at[1], far_recv.at[1], far).wait_recv()

    base = (half * (pair_n * (stored_rows // rank_n))).astype(jnp.float32)
    line = jnp.concatenate([slots_own[...], slots_far[...]], axis=1) - base
    line_rows = jnp.broadcast_to(line[0:1, :], (rows, toks))
    row_slot = (lax.broadcasted_iota(jnp.int32, (rows, toks), 0) // rank_n).astype(jnp.float32)
    mask_t = line_rows == row_slot

    wait_pair(0)
    wait_pair(1)
    copies = max(1, 128 // feat_loc)
    span = copies * feat_loc
    mine = x[:, :, :, pl.ds(pl.multiple_of(k // copies * span, span), span)].reshape(toks, span)
    for i, a_ref in enumerate((ga, ua)):
        a = a_ref[...].reshape(rows, feat_loc)
        if copies > 1:
            a = jnp.concatenate([a] * copies, axis=1)
            part = lax.broadcasted_iota(jnp.int32, (rows, span), 1) // feat_loc
            a = jnp.where(part == lax.rem(k, copies), a, jnp.zeros_like(a))
        low = mm(a, mine, NT)
        low = jnp.where(mask_t, low, 0.0).reshape(slots_n, rank_n, toks)
        mid_own[pl.ds(i * rank_n, rank_n), :] = jnp.sum(low, axis=0).astype(jnp.bfloat16)
    for d in range(1, tensor_n):
        send(mid_own, mid_in.at[d - 1], mid_send.at[d - 1], mid_recv.at[d - 1], peer(d))

    weights[0].wait()
    weights[1].wait()

    def project(cols):
        taken = x[...].reshape(toks, width)
        pre_g[:, cols] = mm(taken, wg[cols, :], NT)
        pre_u[:, cols] = mm(taken, wu[cols, :], NT)

    tiles(hidden_local, project)

    mid = mid_own[...].astype(jnp.float32)
    for d in range(1, tensor_n):
        remote(
            mid_own, mid_in.at[d - 1], mid_send.at[d - 1], mid_recv.at[d - 1], peer(d)
        ).wait_recv()
        mid = mid + mid_in[d - 1].astype(jnp.float32)
    mid = mid.astype(jnp.bfloat16).astype(jnp.float32)
    spreads = []
    for i in range(2):
        part = mid[i * rank_n : (i + 1) * rank_n][None]
        part = jnp.broadcast_to(part, (slots_n, rank_n, toks)).reshape(rows, toks)
        part = jnp.where(mask_t, adapter_scale * part, 0.0)
        spreads.append(part.T.astype(jnp.bfloat16))
    slot_cols = line_rows[: min(rows, 128)].T[:, 0:1]
    held = jnp.logical_and(slot_cols >= 0.0, slot_cols < float(slots_n))
    wait_pair(2)
    wait_pair(3)

    def activate(cols):
        wide = cols.size
        g = pre_g[:, cols] + mm(spreads[0], gb[:, :, cols].reshape(rows, wide), NN)
        u = pre_u[:, cols] + mm(spreads[1], ub[:, :, cols].reshape(rows, wide), NN)
        h = g / (1.0 + jnp.exp(-g)) * u
        hidden[:, cols] = jnp.where(held, h, 0.0).astype(jnp.bfloat16)

    tiles(hidden_local, activate)

    wait_pair(4)
    own_copies[last].wait()
    for d in range(1, pair_n):
        origin = lax.rem(place - d + pair_n, pair_n)
        remote(*half_of(origin, d, own_share)).wait_recv()
        send(*handed(origin, d, own_share))
    low = mm(hidden[...], da[...].reshape(rows, hidden_local), NT)
    col_slot = (lax.broadcasted_iota(jnp.int32, (toks, rows), 1) // rank_n).astype(jnp.float32)
    low = jnp.where(slot_cols == col_slot, adapter_scale * low, 0.0).astype(jnp.bfloat16)
    for d in range(1, pair_n):
        origin = lax.rem(place - d + pair_n, pair_n)
        remote(*handed(origin, d, other_share)).wait_recv()
    weights[2].wait()

    def to_sibling(c):
        cols = pl.ds(c * chunk, chunk)
        return (
            y.at[:, :, 1 - core, :, cols],
            y_pair.at[:, :, :, cols],
            pair_send.at[c],
            pair_recv.at[c],
            sibling,
        )

    def to_chip(c, d):
        cols = pl.ds(c * chunk, chunk)
        return (
            y_sum.at[:, chip_after(d), :, cols],
            y_in.at[d - 1, :, :, cols],
            y_send.at[c, d - 1],
            y_recv.at[c, d - 1],
            across(d),
        )

    def join(c):
        cols = pl.ds(c * chunk, chunk)
        remote(*to_sibling(c)).wait_recv()
        both = y[:, :, core, :, cols].astype(jnp.float32) + y_pair[:, :, :, cols].astype(jnp.float32)
        y_sum[:, :, :, cols] = both.astype(jnp.bfloat16)
        for d in range(1, chips):
            send(*to_chip(c, d))

    for c in range(SUM_CHUNKS):
        cols = pl.ds(c * chunk, chunk)
        part = mm(hidden[...], wd[:, cols], NN) + mm(low, db[:, :, cols].reshape(rows, chunk), NN)
        y[:, :, :, :, cols] = part.astype(jnp.bfloat16).reshape(2, chips, 2, tok_dev, chunk)
        send(*to_sibling(c))
        if c:
            join(c - 1)
    join(SUM_CHUNKS - 1)
    for c in range(SUM_CHUNKS):
        cols = pl.ds(c * chunk, chunk)
        total = y_sum[:, chip, :, cols].astype(jnp.float32)
        for d in range(1, chips):
            remote(*to_chip(c, d)).wait_recv()
            total = total + y_in[d - 1, :, :, cols].astype(jnp.float32)
        z_out[c] = total[1].astype(jnp.bfloat16)
        send(z_out.at[c], z_in.at[c], far_send.at[2 + c], far_recv.at[2 + c], far)
        kept[:, cols] = total[0]
    for c in range(SUM_CHUNKS):
        cols = pl.ds(c * chunk, chunk)
        remote(z_out.at[c], z_in.at[c], far_send.at[2 + c], far_recv.at[2 + c], far).wait_recv()
        whole = resid_ref[:, cols].astype(jnp.float32) + kept[:, cols] + z_in[c].astype(jnp.float32)
        out_ref[:, cols] = whole.astype(jnp.bfloat16)
    for copy in sends:
        copy.wait_send()


def local(
    pair_n,
    resid,
    norm_gain,
    gate_weight_matrix,
    up_weight,
    w_down,
    gate_a,
    gate_b,
    up_a,
    up_b,
    down_a,
    down_b,
    prompt_lengths,
    prompt_choice,
    used_adapters,
    adapter_holder,
):
    tensor_n = lax.axis_size("tensor")
    _, tok_dev, width = resid.shape
    stored, feat_loc, rank_n = gate_a.shape
    hidden_local = gate_weight_matrix.shape[1]
    toks = 2 * tok_dev * tensor_n
    rows = stored * rank_n
    bf = jnp.bfloat16

    def by_row(a):
        return jnp.transpose(a, (0, 2, 1)).reshape(rows, a.shape[1])

    def flat(b):
        return b.reshape(rows, b.shape[2])

    vmem = pl.BlockSpec(memory_space=pltpu.VMEM)
    smem = pl.BlockSpec(memory_space=pltpu.SMEM)
    hbm = pl.BlockSpec(memory_space=pl.ANY)
    dma = pltpu.SemaphoreType.DMA
    chunk = width // SUM_CHUNKS
    out = pl.pallas_call(
        functools.partial(kernel, tensor_n, pair_n),
        out_shape=jax.ShapeDtypeStruct((tok_dev, width), bf),
        in_specs=[vmem, vmem, hbm, hbm, hbm] + [vmem] * 6 + [smem] * 4,
        out_specs=vmem,
        scratch_shapes=[
            pltpu.VMEM((hidden_local, width), bf),
            pltpu.VMEM((hidden_local, width), bf),
            pltpu.VMEM((hidden_local, width), bf),
            pltpu.VMEM((2, tensor_n, tok_dev, width), bf),
            pltpu.VMEM((pair_n, rows, feat_loc), bf),
            pltpu.VMEM((pair_n, rows, hidden_local), bf),
            pltpu.VMEM((pair_n, rows, feat_loc), bf),
            pltpu.VMEM((pair_n, rows, hidden_local), bf),
            pltpu.VMEM((pair_n, rows, hidden_local), bf),
            pltpu.VMEM((pair_n, rows, width), bf),
            pltpu.VMEM((8, toks // 2), jnp.float32),
            pltpu.VMEM((8, toks // 2), jnp.float32),
            pltpu.VMEM((2 * rank_n, toks), bf),
            pltpu.VMEM((tensor_n - 1, 2 * rank_n, toks), bf),
            pltpu.VMEM((toks, hidden_local), jnp.float32),
            pltpu.VMEM((toks, hidden_local), jnp.float32),
            pltpu.VMEM((toks, hidden_local), bf),
            pltpu.VMEM((2, tensor_n // 2, 2, tok_dev, width), bf),
            pltpu.VMEM((2, tensor_n // 2, tok_dev, width), bf),
            pltpu.VMEM((2, tensor_n // 2, tok_dev, width), bf),
            pltpu.VMEM((tensor_n // 2 - 1, 2, tok_dev, width), bf),
            pltpu.VMEM((SUM_CHUNKS, tok_dev, chunk), bf),
            pltpu.VMEM((SUM_CHUNKS, tok_dev, chunk), bf),
            pltpu.VMEM((tok_dev, width), jnp.float32),
            dma((3,)),
            dma((6,)),
            dma((2, tensor_n - 1)),
            dma((2, tensor_n - 1)),
            dma((2 + SUM_CHUNKS,)),
            dma((2 + SUM_CHUNKS,)),
            dma((7, max(1, pair_n - 1))),
            dma((7, max(1, pair_n - 1))),
            dma((tensor_n - 1,)),
            dma((tensor_n - 1,)),
            dma((SUM_CHUNKS, tensor_n // 2 - 1)),
            dma((SUM_CHUNKS, tensor_n // 2 - 1)),
            dma((SUM_CHUNKS,)),
            dma((SUM_CHUNKS,)),
        ],
        compiler_params=pltpu.CompilerParams(
            collective_id=0, has_side_effects=True, vmem_limit_bytes=60 * 2**20
        ),
        name="ffn",
    )(
        resid[0],
        norm_gain[None],
        gate_weight_matrix.T,
        up_weight.T,
        w_down,
        by_row(gate_a),
        flat(gate_b),
        by_row(up_a),
        flat(up_b),
        by_row(down_a),
        flat(down_b),
        prompt_lengths,
        prompt_choice,
        used_adapters,
        adapter_holder,
    )
    return out[None]


def solution(mesh):
    placed = (
        P("seq", "tensor", None),
        P(),
        P(None, "tensor"),
        P(None, "tensor"),
        P("tensor", None),
        P("seq", "tensor", None),
        P("seq", None, "tensor"),
        P("seq", "tensor", None),
        P("seq", None, "tensor"),
        P("seq", "tensor", None),
        P("seq", None, None),
        P("seq", None),
        P("seq", None),
        P(),
        P(),
    )
    return jax.shard_map(
        functools.partial(local, mesh.shape["seq"] // 2),
        mesh=mesh,
        in_specs=placed,
        out_specs=P("seq", "tensor", None),
        check_vma=False,
    )
```
